32 devices in a mesh: ctx: 16 (over z, y, x), head: 2 (over core).
Axes of the slice: x: 2, y: 2, z: 4, core: 2. Of those that a mesh axis runs over, the one named last changes fastest.
Arguments:
- queries: bfloat16 [4096, 4096], P('ctx', 'head'), may hold values from -15 to 15
- key_rows: bfloat16 [4096, 4096], P('ctx', 'head'), may hold values from -4 to 4
- value_rows: bfloat16 [4096, 4096], P('ctx', 'head'), may hold values from -32 to 32
- cotangent: bfloat16 [4096, 4096], P('ctx', 'head'), may hold values from -6 to 6
- norm_gain: float32 [4096], P('head'), may hold values from 0.1 to 1.9
- pairing: int32 [16], replicated, may hold values from 0 to 15, as said below
Outputs:
- mixed: bfloat16 [4096, 4096], P('ctx', 'head')
- grad_query: bfloat16 [4096, 4096], P('ctx', 'head')
- grad_key: bfloat16 [4096, 4096], P('ctx', 'head')
- grad_value: bfloat16 [4096, 4096], P('ctx', 'head')
The draws below stay inside these ranges and needn't reach their ends.
Inputs may be any that keep to these rules, and one draw needn't show every extreme that they name: pairing is a permutation of the 16 blocks, and pairing[b] differs from b.
All inputs are finite; a program needn't handle non-finite values.
Results may differ from the reference program's by a relative error of at most 0.012.
Values may be sent and summed in bfloat16 or wider, within the bound.
No kernel may reach another device: no remote copies, remote signals or barrier semaphores. Data moves between devices by JAX's collectives and lax.ppermute only.
A program may use at most 64 MiB of HBM per device.

```python
import math
import jax
import jax.numpy as jnp
from jax import lax

H = 32
HD = 128
BLOCK = 256
BLK_DEV = 1
BLOCKS = 16
TOKENS = 4096


def query_key_pair(base):
    folded = jax.random.fold_in(base, 11)
    streams = jax.random.split(folded, 2)
    width = H * HD
    drawn_query = jnp.clip(jax.random.normal(streams[0], (TOKENS, width), jnp.float32), -4.0, 4.0) * 2.0
    drawn_key = jnp.clip(jax.random.normal(streams[1], (TOKENS, width), jnp.float32), -4.0, 4.0)
    return (drawn_query, drawn_key)


def draw_queries(key, part):
    return query_key_pair(key)[0].astype(jnp.bfloat16)


def draw_key_rows(key, part):
    return query_key_pair(key)[1].astype(jnp.bfloat16)


def draw_value_rows(key, part):
    width = H * HD
    folded = jax.random.fold_in(key, 23)
    heads_of = (jnp.arange(width) // HD).astype(jnp.float32) / (H - 1)
    column_scale = 3.0 ** heads_of
    base_values = jnp.clip(jax.random.normal(folded, (TOKENS, width), jnp.float32), -4.0, 4.0)
    return (2.0 * base_values * column_scale[None, :]).astype(jnp.bfloat16)


def draw_pairing(key, part):
    devices = BLOCKS // BLK_DEV
    folded = jax.random.fold_in(key, 5)
    streams = jax.random.split(folded, BLK_DEV + 1)
    targets = []
    for column in range(BLK_DEV):
        cycle = jax.random.permutation(streams[column], devices).astype(jnp.int32)
        follow = jnp.zeros((devices,), jnp.int32).at[cycle].set(jnp.roll(cycle, -1))
        targets.append(follow)
    target = jnp.stack(targets, axis=1)
    ranking = jax.random.randint(streams[BLK_DEV], (devices, BLK_DEV), 0, 1 << 20) * BLK_DEV + jnp.arange(BLK_DEV, dtype=jnp.int32)[None, :]
    slots = jnp.argsort(ranking, axis=1).astype(jnp.int32)
    column_ids = jnp.broadcast_to(jnp.arange(BLK_DEV, dtype=jnp.int32)[None, :], (devices, BLK_DEV))
    landing = slots[target, column_ids]
    return (target * BLK_DEV + landing).reshape(-1).astype(jnp.int32)


def block_scale(stream_key, shape, pieces, least, largest):
    def one(dim, shards_of):
        draws = jax.random.uniform(jax.random.fold_in(jax.random.fold_in(stream_key, 6), dim), (shards_of,), jnp.float32, least / len(pieces), largest / len(pieces))
        return jnp.repeat(jnp.exp(draws), shape[dim] // shards_of).reshape((-1,) + (1,) * (len(shape) - dim - 1))

    gain = one(*pieces[0])
    for cut in pieces[1:]:
        gain = gain * one(*cut)
    return gain


def scatter_about(rng, shape, scale, limit, pieces=(), held_as=jnp.bfloat16):
    entries = scale * jax.random.normal(rng, shape, jnp.float32)
    if pieces:
        entries = entries * block_scale(rng, shape, pieces, -0.22, 0.18)
    return jnp.clip(entries, -limit, limit).astype(held_as)


def setup_inputs(seed: int = 0) -> dict:
    splits = jax.random.split(jax.random.key(seed), 7)
    queries = draw_queries(jax.random.fold_in(splits[6], 71), 0)
    key_rows = draw_key_rows(jax.random.fold_in(splits[6], 71), 0)
    value_rows = draw_value_rows(jax.random.fold_in(splits[6], 71), 0)
    cotangent = scatter_about(splits[3], (TOKENS, H * HD), 1.0, 6.0, ((0, 16), (1, 2)))
    norm_gain = jnp.clip(1.0 + 0.18 * jax.random.normal(splits[4], (H * HD,), jnp.float32), 0.1, 1.9)
    pairing = draw_pairing(jax.random.fold_in(splits[6], 71), 0)
    return dict(queries=queries, key_rows=key_rows, value_rows=value_rows, cotangent=cotangent, norm_gain=norm_gain, pairing=pairing)


def reference(queries, key_rows, value_rows, cotangent, norm_gain, pairing):
    f32 = jnp.float32
    bf16 = jnp.bfloat16
    factor = 1.0 / math.sqrt(HD)
    query_blocks = queries.reshape(BLOCKS, BLOCK, H, HD)
    key_blocks = key_rows.reshape(BLOCKS, BLOCK, H, HD)
    value_blocks = value_rows.reshape(BLOCKS, BLOCK, H, HD)
    places = jnp.arange(BLOCK)
    causal = places[:, None] >= places[None, :]

    def window_of(block_id):
        partner = pairing[block_id]
        before = (block_id - 1) % BLOCKS
        keys_here = jnp.concatenate([key_blocks[before], key_blocks[block_id], key_blocks[partner]], axis=0)
        values_here = jnp.concatenate([value_blocks[before], value_blocks[block_id], value_blocks[partner]], axis=0)
        earlier = jnp.broadcast_to(block_id > 0, (BLOCK, BLOCK))
        allowed = jnp.concatenate([earlier, causal, jnp.ones((BLOCK, BLOCK), bool)], axis=1)
        scores = jnp.einsum('ihd,jhd->hij', query_blocks[block_id].astype(f32), keys_here.astype(f32)) * factor
        scores = jnp.where(allowed[None], scores, -jnp.inf)
        return (keys_here, values_here, scores)

    def forward_block(block_id):
        keys_here, values_here, scores = window_of(block_id)
        highest = lax.optimization_barrier(jnp.max(scores, axis=-1, keepdims=True))
        logsum = highest + jnp.log(lax.optimization_barrier(jnp.sum(jnp.exp(scores - highest), axis=-1, keepdims=True)))
        weights = jnp.exp(scores - logsum)
        rounded = lax.optimization_barrier(weights.astype(bf16)).astype(f32)
        attn_block = jnp.einsum('hij,jhd->ihd', rounded, values_here.astype(f32)).astype(bf16)
        return (attn_block, logsum)
    block_ids = jnp.arange(BLOCKS, dtype=jnp.int32)
    attn, logsums = lax.map(forward_block, block_ids)
    attn_flat = attn.reshape(TOKENS, H * HD).astype(f32)
    rms_scale = lax.rsqrt(lax.optimization_barrier(jnp.mean(attn_flat * attn_flat, axis=1, keepdims=True)) + 1e-05)
    mixed = (attn_flat * rms_scale * norm_gain).astype(bf16)
    grad_in = norm_gain * cotangent.astype(f32)
    product_mean = lax.optimization_barrier(jnp.mean(grad_in * attn_flat, axis=1, keepdims=True))
    dattn = (rms_scale * grad_in - attn_flat * rms_scale ** 3 * product_mean).astype(bf16)
    dattn_blocks = dattn.reshape(BLOCKS, BLOCK, H, HD)
    delta = lax.optimization_barrier(jnp.sum(dattn_blocks.astype(f32) * attn.astype(f32), axis=-1))

    def backward_block(block_id):
        keys_here, values_here, scores = window_of(block_id)
        weights = jnp.exp(scores - logsums[block_id])
        rounded = lax.optimization_barrier(weights.astype(bf16)).astype(f32)
        grad_here = dattn_blocks[block_id].astype(f32)
        dprob = jnp.einsum('ihd,jhd->hij', grad_here, values_here.astype(f32))
        dscore = weights * (dprob - jnp.transpose(delta[block_id])[:, :, None])
        dscore = lax.optimization_barrier(dscore.astype(bf16)).astype(f32)
        dquery = (jnp.einsum('hij,jhd->ihd', dscore, keys_here.astype(f32)) * factor).astype(bf16)
        dkey = (jnp.einsum('hij,ihd->jhd', dscore, query_blocks[block_id].astype(f32)) * factor).astype(bf16)
        dvalue = jnp.einsum('hij,ihd->jhd', rounded, grad_here).astype(bf16)
        return (dquery, dkey, dvalue)
    grad_query, key_terms, value_terms = lax.map(backward_block, block_ids)

    def combine(terms):
        before_term = terms[:, :BLOCK]
        own_term = terms[:, BLOCK:2 * BLOCK]
        partner_term = terms[:, 2 * BLOCK:]
        from_next = jnp.roll(before_term, -1, axis=0)
        from_partner = jnp.zeros_like(partner_term).at[pairing].set(partner_term)
        total = own_term.astype(f32) + from_next.astype(f32) + from_partner.astype(f32)
        return total.astype(bf16).reshape(TOKENS, H * HD)
    return (mixed, grad_query.reshape(TOKENS, H * HD), combine(key_terms), combine(value_terms))
```

```python
import functools
import math

import jax
import jax.numpy as jnp
from jax import lax
from jax.experimental import pallas as pl
from jax.experimental.pallas import tpu as pltpu
from jax.sharding import PartitionSpec as P

HEADS = 32
HD = 128
BLOCK = 256
EPSILON = 1e-05
FACTOR = 1.0 / math.sqrt(HD)
LOG2E = math.log2(math.e)
MASKED = -1e30
F32 = jnp.float32
BF16 = jnp.bfloat16


def dot(a, b, contract):
    return lax.dot_general(a, b, (contract, ((), ())), preferred_element_type=F32)


NT = ((1,), (1,))
NN = ((1,), (0,))
TN = ((0,), (0,))


def head(h):
    return pl.ds(h * HD, HD)


def scores_kernel(group, index_ref, q, kp, ko, kt, vp, vo, pp_out, po_out, pt_out, acc_out):
    first = index_ref[0] == 0
    rows = lax.broadcasted_iota(jnp.int32, (BLOCK, BLOCK), 0)
    cols = lax.broadcasted_iota(jnp.int32, (BLOCK, BLOCK), 1)
    causal = rows >= cols
    for h in range(group):
        here = q[:, head(h)]
        scale = FACTOR * LOG2E
        sp = jnp.where(first, MASKED, dot(here, kp[:, head(h)], NT) * scale)
        so = jnp.where(causal, dot(here, ko[:, head(h)], NT) * scale, MASKED)
        st = dot(here, kt[:, head(h)], NT) * scale
        top = jnp.max(jnp.maximum(jnp.maximum(sp, so), st), axis=1, keepdims=True)
        ep = jnp.exp2(sp - top)
        eo = jnp.exp2(so - top)
        et = jnp.exp2(st - top)
        inverse = 1.0 / jnp.sum(ep + eo + et, axis=1, keepdims=True)
        wp = (ep * inverse).astype(BF16)
        wo = (eo * inverse).astype(BF16)
        pp_out[h] = wp
        po_out[h] = wo
        pt_out[h] = (et * inverse).astype(BF16)
        acc_out[:, head(h)] = dot(wp, vp[:, head(h)], NN) + dot(wo, vo[:, head(h)], NN)


def attn_kernel(group, steps, pt, vt, acc, cot, gain, attn_out, sums_out, square, product):
    step = pl.program_id(0)

    @pl.when(step == 0)
    def _():
        square[...] = jnp.zeros_like(square)
        product[...] = jnp.zeros_like(product)

    sq = square[...]
    pr = product[...]
    for h in range(group):
        low = (acc[:, head(h)] + dot(pt[h], vt[:, head(h)], NN)).astype(BF16)
        attn_out[:, head(h)] = low
        wide = low.astype(F32)
        sq = sq + wide * wide
        pr = pr + gain[:, head(h)] * cot[:, head(h)].astype(F32) * wide
    square[...] = sq
    product[...] = pr

    @pl.when(step == steps - 1)
    def _():
        sums_out[0:1, :] = jnp.sum(jnp.transpose(square[...]), axis=0, keepdims=True)
        sums_out[1:2, :] = jnp.sum(jnp.transpose(product[...]), axis=0, keepdims=True)


def norm_terms(sums, features):
    table = jnp.concatenate([sums[...], jnp.zeros((6, BLOCK), F32)], axis=0)
    columns = jnp.transpose(table)
    rms = lax.rsqrt(columns[:, 0:1] / features + EPSILON)
    return rms, columns[:, 1:2] / features


def dattn_kernel(group, features, sums, attn, cot, gain, pt, dattn_out, dvt_out):
    rms, mean = norm_terms(sums, features)
    back = rms * rms * rms * mean
    for h in range(group):
        grad_in = gain[:, head(h)] * cot[:, head(h)].astype(F32)
        low = (rms * grad_in - attn[:, head(h)].astype(F32) * back).astype(BF16)
        dattn_out[:, head(h)] = low
        dvt_out[:, head(h)] = dot(pt[h], low, TN).astype(BF16)


def dscore_of(weights, dattn, attn, values):
    delta = jnp.sum(dattn.astype(F32) * attn.astype(F32), axis=1, keepdims=True)
    return (weights.astype(F32) * (dot(dattn, values, NT) - delta)).astype(BF16)


def partner_kernel(group, pt, dattn, attn, vt, kt, q, dkt_out, dq_out):
    for h in range(group):
        ds = dscore_of(pt[h], dattn[:, head(h)], attn[:, head(h)], vt[:, head(h)])
        dkt_out[:, head(h)] = (dot(ds, q[:, head(h)], TN) * FACTOR).astype(BF16)
        dq_out[:, head(h)] = dot(ds, kt[:, head(h)], NN)


def prior_kernel(group, pp, dattn, attn, vp, kp, q, dq_in, dvp_out, dkp_out, dq_out):
    for h in range(group):
        low = dattn[:, head(h)]
        ds = dscore_of(pp[h], low, attn[:, head(h)], vp[:, head(h)])
        dvp_out[:, head(h)] = dot(pp[h], low, TN).astype(BF16)
        dkp_out[:, head(h)] = (dot(ds, q[:, head(h)], TN) * FACTOR).astype(BF16)
        dq_out[:, head(h)] = dq_in[:, head(h)] + dot(ds, kp[:, head(h)], NN)


def own_kernel(group, features, sums, po, dattn, attn, vo, ko, q, dq_in, gain, dvo_out, dko_out, dq_out, mixed_out):
    rms, _ = norm_terms(sums, features)
    for h in range(group):
        low = dattn[:, head(h)]
        ds = dscore_of(po[h], low, attn[:, head(h)], vo[:, head(h)])
        dvo_out[:, head(h)] = dot(po[h], low, TN).astype(BF16)
        dko_out[:, head(h)] = (dot(ds, q[:, head(h)], TN) * FACTOR).astype(BF16)
        dq_out[:, head(h)] = ((dq_in[:, head(h)] + dot(ds, ko[:, head(h)], NN)) * FACTOR).astype(BF16)
        mixed_out[:, head(h)] = (attn[:, head(h)].astype(F32) * rms * gain[:, head(h)]).astype(BF16)


def from_behind(value, steps):
    count = lax.axis_size("ctx")
    first, last = (max(0, -steps), min(count, count - steps))
    return lax.ppermute(value, "ctx", [(source, source + steps) for source in range(first, last)])


def exchange(pieces):
    return lax.all_to_all(pieces, "ctx", split_axis=0, concat_axis=0, tiled=True)


def spread(value):
    devices = lax.axis_size("ctx")
    return exchange(value.reshape(devices, value.shape[0] // devices, value.shape[1]))


def collect(pieces, wanted):
    chosen = jnp.take(pieces, wanted, axis=0, mode="clip")
    return exchange(chosen).reshape(pieces.shape[0] * pieces.shape[1], pieces.shape[2])


def on_device(queries, key_rows, value_rows, cotangent, norm_gain, pairing):
    width = queries.shape[1]
    heads = width // HD
    group = math.gcd(4, heads)
    steps = heads // group
    features = float(HEADS * HD)
    wide = pl.BlockSpec((BLOCK, group * HD), lambda g: (0, g))
    square = pl.BlockSpec((group, BLOCK, BLOCK), lambda g: (g, 0, 0))
    line = pl.BlockSpec((1, group * HD), lambda g: (0, g))
    whole = pl.BlockSpec((2, BLOCK), lambda g: (0, 0))
    rows_low = jax.ShapeDtypeStruct((BLOCK, width), BF16)
    rows_wide = jax.ShapeDtypeStruct((BLOCK, width), F32)
    weights = jax.ShapeDtypeStruct((heads, BLOCK, BLOCK), BF16)

    def call(body, name, ins, outs, shapes, dots, exps=0, scratch=()):
        return pl.pallas_call(
            body,
            name=name,
            grid=(steps,),
            in_specs=ins,
            out_specs=outs,
            out_shape=shapes,
            scratch_shapes=scratch,
            compiler_params=pltpu.CompilerParams(vmem_limit_bytes=32 * 2**20),
            cost_estimate=pl.CostEstimate(
                flops=dots * heads * 2 * BLOCK * BLOCK * HD,
                bytes_accessed=(len(ins) + len(outs)) * BLOCK * width * 2,
                transcendentals=exps * heads * BLOCK * BLOCK,
            ),
        )

    gain = norm_gain.reshape(1, width)
    index = lax.axis_index("ctx").astype(jnp.int32).reshape(1)
    numbers = jnp.arange(pairing.shape[0], dtype=jnp.int32)
    inverse = jnp.sum(
        jnp.where(pairing[None, :] == numbers[:, None], numbers[None, :], 0), axis=1
    )

    kp = from_behind(key_rows, 1)
    vp = from_behind(value_rows, 1)
    keys_spread = spread(key_rows)
    values_spread = spread(value_rows)
    kt = collect(keys_spread, pairing)
    vt = collect(values_spread, pairing)

    smem = pl.BlockSpec(memory_space=pltpu.SMEM)
    pp, po, pt, acc = call(
        functools.partial(scores_kernel, group),
        "scores",
        [smem] + [wide] * 6,
        [square] * 3 + [wide],
        [weights] * 3 + [rows_wide],
        5,
        3,
    )(index, queries, kp, key_rows, kt, vp, value_rows)
    attn, sums = call(
        functools.partial(attn_kernel, group, steps),
        "attn",
        [square, wide, wide, wide, line],
        [wide, whole],
        [rows_low, jax.ShapeDtypeStruct((2, BLOCK), F32)],
        1,
        scratch=[pltpu.VMEM((BLOCK, HD), F32)] * 2,
    )(pt, vt, acc, cotangent, gain)
    sums = lax.psum(sums, "head")
    dattn, dvt = call(
        functools.partial(dattn_kernel, group, features),
        "dattn",
        [whole, wide, wide, line, square],
        [wide, wide],
        [rows_low] * 2,
        1,
    )(sums, attn, cotangent, gain, pt)
    dvt_spread = spread(dvt)
    dkt, dq = call(
        functools.partial(partner_kernel, group),
        "partner",
        [square] + [wide] * 5,
        [wide, wide],
        [rows_low, rows_wide],
        3,
    )(pt, dattn, attn, vt, kt, queries)
    dkt_spread = spread(dkt)
    dvp, dkp, dq = call(
        functools.partial(prior_kernel, group),
        "prior",
        [square] + [wide] * 6,
        [wide] * 3,
        [rows_low, rows_low, rows_wide],
        4,
    )(pp, dattn, attn, vp, kp, queries, dq)
    dvn = from_behind(dvp, -1)
    dkn = from_behind(dkp, -1)
    dvo, dko, grad_query, mixed = call(
        functools.partial(own_kernel, group, features),
        "own",
        [whole, square] + [wide] * 6 + [line],
        [wide] * 4,
        [rows_low] * 4,
        4,
    )(sums, po, dattn, attn, value_rows, key_rows, queries, dq, gain)
    dvt_home = collect(dvt_spread, inverse)
    dkt_home = collect(dkt_spread, inverse)
    grad_value = (dvo.astype(F32) + dvn.astype(F32) + dvt_home.astype(F32)).astype(BF16)
    grad_key = (dko.astype(F32) + dkn.astype(F32) + dkt_home.astype(F32)).astype(BF16)
    return mixed, grad_query, grad_key, grad_value


def solution(mesh):
    rows = P("ctx", "head")
    return jax.shard_map(
        on_device,
        mesh=mesh,
        in_specs=(rows, rows, rows, rows, P("head"), P()),
        out_specs=(rows, rows, rows, rows),
        check_vma=False,
    )
```

```python
import functools
import math

import jax
import jax.numpy as jnp
from jax import lax
from jax.experimental import pallas as pl
from jax.experimental.pallas import tpu as pltpu
from jax.sharding import PartitionSpec as P

HEADS = 32
HD = 128
BLOCK = 256
EPSILON = 1e-05
FACTOR = 1.0 / math.sqrt(HD)
LOG2E = math.log2(math.e)
MASKED = -1e30
F32 = jnp.float32
BF16 = jnp.bfloat16


def dot(a, b, contract):
    return lax.dot_general(a, b, (contract, ((), ())), preferred_element_type=F32)


NT = ((1,), (1,))
NN = ((1,), (0,))
TN = ((0,), (0,))


def head(h):
    return pl.ds(h * HD, HD)


def joined(parts, h):
    return jnp.concatenate([part[:, head(h)] for part in parts], axis=0)


def scores_kernel(group, index_ref, q, ko, kt, vo, *rest):
    kp = rest[:-4]
    pp_out, po_out, pt_out, acc_out = rest[-4:]
    first = index_ref[0] == 0
    rows = lax.broadcasted_iota(jnp.int32, (BLOCK, BLOCK), 0)
    cols = lax.broadcasted_iota(jnp.int32, (BLOCK, BLOCK), 1)
    causal = rows >= cols
    for h in range(group):
        here = q[:, head(h)]
        scale = FACTOR * LOG2E
        sp = jnp.where(first, MASKED, dot(here, joined(kp, h), NT) * scale)
        so = jnp.where(causal, dot(here, ko[:, head(h)], NT) * scale, MASKED)
        st = dot(here, kt[:, head(h)], NT) * scale
        top = jnp.max(jnp.maximum(jnp.maximum(sp, so), st), axis=1, keepdims=True)
        ep = jnp.exp2(sp - top)
        eo = jnp.exp2(so - top)
        et = jnp.exp2(st - top)
        inverse = 1.0 / jnp.sum(ep + eo + et, axis=1, keepdims=True)
        wo = (eo * inverse).astype(BF16)
        pp_out[h] = (ep * inverse).astype(BF16)
        po_out[h] = wo
        pt_out[h] = (et * inverse).astype(BF16)
        acc_out[:, head(h)] = dot(wo, vo[:, head(h)], NN)


def attn_kernel(group, steps, pp, pt, vt, acc, cot, gain, *rest):
    vp = rest[:-4]
    attn_out, sums_out, square, product = rest[-4:]
    step = pl.program_id(0)

    @pl.when(step == 0)
    def _():
        square[...] = jnp.zeros_like(square)
        product[...] = jnp.zeros_like(product)

    sq = square[...]
    pr = product[...]
    for h in range(group):
        total = acc[:, head(h)] + dot(pp[h], joined(vp, h), NN)
        low = (total + dot(pt[h], vt[:, head(h)], NN)).astype(BF16)
        attn_out[:, head(h)] = low
        wide = low.astype(F32)
        sq = sq + wide * wide
        pr = pr + gain[:, head(h)] * cot[:, head(h)].astype(F32) * wide
    square[...] = sq
    product[...] = pr

    @pl.when(step == steps - 1)
    def _():
        sums_out[0:1, :] = jnp.sum(jnp.transpose(square[...]), axis=0, keepdims=True)
        sums_out[1:2, :] = jnp.sum(jnp.transpose(product[...]), axis=0, keepdims=True)


def norm_terms(sums, features):
    table = jnp.concatenate([sums[...], jnp.zeros((6, BLOCK), F32)], axis=0)
    columns = jnp.transpose(table)
    rms = lax.rsqrt(columns[:, 0:1] / features + EPSILON)
    return rms, columns[:, 1:2] / features


def dattn_kernel(group, features, sums, attn, cot, gain, pt, dattn_out, dvt_out):
    rms, mean = norm_terms(sums, features)
    back = rms * rms * rms * mean
    for h in range(group):
        grad_in = gain[:, head(h)] * cot[:, head(h)].astype(F32)
        low = (rms * grad_in - attn[:, head(h)].astype(F32) * back).astype(BF16)
        dattn_out[:, head(h)] = low
        dvt_out[:, head(h)] = dot(pt[h], low, TN).astype(BF16)


def dscore_of(weights, dattn, attn, values):
    delta = jnp.sum(dattn.astype(F32) * attn.astype(F32), axis=1, keepdims=True)
    return (weights.astype(F32) * (dot(dattn, values, NT) - delta)).astype(BF16)


def partner_kernel(group, pt, dattn, attn, vt, kt, q, dq_in, dkt_out, dq_out):
    for h in range(group):
        ds = dscore_of(pt[h], dattn[:, head(h)], attn[:, head(h)], vt[:, head(h)])
        dkt_out[:, head(h)] = (dot(ds, q[:, head(h)], TN) * FACTOR).astype(BF16)
        dq_out[:, head(h)] = dq_in[:, head(h)] + dot(ds, kt[:, head(h)], NN)


def prior_kernel(group, pp, dattn, attn, q, *rest):
    dvp_out, dkp_out, dq_out = rest[-3:]
    vp, kp = rest[:2], rest[2:4]
    for h in range(group):
        low = dattn[:, head(h)]
        ds = dscore_of(pp[h], low, attn[:, head(h)], joined(vp, h))
        dvp_out[:, head(h)] = dot(pp[h], low, TN).astype(BF16)
        dkp_out[:, head(h)] = (dot(ds, q[:, head(h)], TN) * FACTOR).astype(BF16)
        dq_out[:, head(h)] = dot(ds, joined(kp, h), NN)


def finish_kernel(own, home, near_upper, near_lower, out):
    near = jnp.concatenate([near_upper[...], near_lower[...]], axis=0).astype(F32)
    out[...] = (own[...].astype(F32) + near + home[...].astype(F32)).astype(BF16)


def own_kernel(group, features, sums, po, dattn, attn, vo, ko, q, dq_in, gain, dvo_out, dko_out, dq_out, mixed_out):
    rms, _ = norm_terms(sums, features)
    for h in range(group):
        low = dattn[:, head(h)]
        ds = dscore_of(po[h], low, attn[:, head(h)], vo[:, head(h)])
        dvo_out[:, head(h)] = dot(po[h], low, TN).astype(BF16)
        dko_out[:, head(h)] = (dot(ds, q[:, head(h)], TN) * FACTOR).astype(BF16)
        dq_out[:, head(h)] = ((dq_in[:, head(h)] + dot(ds, ko[:, head(h)], NN)) * FACTOR).astype(BF16)
        mixed_out[:, head(h)] = (attn[:, head(h)].astype(F32) * rms * gain[:, head(h)]).astype(BF16)


def shift(value, steps):
    count = lax.axis_size("ctx")
    first, last = (max(0, -steps), min(count, count - steps))
    return lax.ppermute(value, "ctx", [(source, source + steps) for source in range(first, last)])


def upper(value):
    return value[: value.shape[0] // 2]


def lower(value):
    return value[value.shape[0] // 2 :]


def half_exchange(pieces):
    count = lax.axis_size("ctx")
    half = count // 2
    groups = [list(range(half)), list(range(half, count))]
    return lax.all_to_all(
        pieces, "ctx", split_axis=0, concat_axis=0, tiled=True, axis_index_groups=groups
    )


def spread(value):
    half = lax.axis_size("ctx") // 2
    return half_exchange(value.reshape(half, value.shape[0] // half, value.shape[1]))


def collect(pieces):
    return half_exchange(pieces).reshape(pieces.shape[0] * pieces.shape[1], pieces.shape[2])


def plan_kernel(count, unit, index, pairing, *refs):
    half = count // 2
    inverse, rank = refs[-2:]
    base = jnp.where(index[0] >= half, half, 0)

    def invert(block, carry):
        inverse[pairing[block]] = block
        return carry

    lax.fori_loop(0, count, invert, 0)
    for way, (wanted, holders) in enumerate(((pairing, inverse), (inverse, pairing))):
        level, order, pick = refs[3 * way : 3 * way + 3]

        def clear(slot, carry):
            order[slot] = 0
            return carry

        def number(block, total):
            leaves = (holders[block] >= half) != (block >= half)
            rank[block] = total

            @pl.when(leaves & (block >= base) & (block < base + half))
            def _():
                order[total] = block - base

            return total + leaves.astype(jnp.int32)

        def place(slot, carry):
            source = wanted[base + slot]
            inside = (source >= base) & (source < base + half)
            pick[slot] = jnp.where(inside, source - base, half + rank[source])
            return carry

        lax.fori_loop(0, half, clear, 0)
        total = lax.fori_loop(0, half, number, jnp.int32(0))
        lax.fori_loop(half, count, number, jnp.int32(0))
        lax.fori_loop(0, half, place, 0)
        level[0] = (total + unit - 1) // unit


def make_plans(index, pairing):
    count = pairing.shape[0]
    half = count // 2
    smem = pl.BlockSpec(memory_space=pltpu.SMEM)
    shapes = [jax.ShapeDtypeStruct((size,), jnp.int32) for size in (1, half, half)]
    plans = pl.pallas_call(
        functools.partial(plan_kernel, count, -(-half // 8)),
        name="plan",
        in_specs=[smem, smem],
        out_specs=[smem] * 6,
        out_shape=shapes * 2,
        scratch_shapes=[pltpu.SMEM((count,), jnp.int32)] * 2,
    )(index, pairing)
    return plans[:3], plans[3:]


def pick_kernel(half, pick, pieces, *rest):
    out, sems = rest[-2:]
    size = out.shape[0]
    for t in range(size):
        index = pick[t]
        if len(rest) == 2:
            pltpu.make_async_copy(pieces.at[index], out.at[t], sems.at[t]).start()
            continue

        @pl.when(index < half)
        def _():
            pltpu.make_async_copy(pieces.at[index], out.at[t], sems.at[t]).start()

        @pl.when(index >= half)
        def _():
            pltpu.make_async_copy(rest[0].at[index - half], out.at[t], sems.at[t]).start()

    for t in range(size):
        pltpu.make_async_copy(pieces.at[0], out.at[t], sems.at[t]).wait()


def pick_pieces(pick, size, *sources):
    half = sources[0].shape[0]
    shape = (size,) + sources[0].shape[1:]
    return pl.pallas_call(
        functools.partial(pick_kernel, half),
        name="pick",
        in_specs=[pl.BlockSpec(memory_space=pltpu.SMEM)]
        + [pl.BlockSpec(memory_space=pl.ANY)] * len(sources),
        out_specs=pl.BlockSpec(memory_space=pltpu.VMEM),
        out_shape=jax.ShapeDtypeStruct(shape, sources[0].dtype),
        scratch_shapes=[pltpu.SemaphoreType.DMA((size,))],
        cost_estimate=pl.CostEstimate(
            flops=0, bytes_accessed=4 * math.prod(shape), transcendentals=0
        ),
    )(pick, *sources)


def cross(pieces, plan, beside, extras):
    level, order, pick = plan
    count = lax.axis_size("ctx")
    half = count // 2
    unit = -(-half // 8)
    pairs = [(i, (i + half) % count) for i in range(count)]

    def branch(number):
        size = min(number * unit, half)

        def run(pieces, order, pick, *extras):
            sources = [pieces]
            if size:
                leaving = pick_pieces(order, size, pieces)
                leaving, *extras = lax.optimization_barrier((leaving, *extras))
                sources.append(lax.ppermute(leaving, "ctx", pairs))
            moved = beside(*extras)
            return pick_pieces(pick, half, *sources), moved

        return run

    levels = -(-half // unit) + 1
    return lax.switch(
        level[0],
        [branch(number) for number in range(levels)],
        pieces,
        order,
        pick,
        *extras,
    )


def stage(pairing, body, *args):
    shapes = jax.eval_shape(body, *args)

    def empty(*args):
        return jax.tree.map(lambda leaf: jnp.zeros(leaf.shape, leaf.dtype), shapes)

    return lax.cond(pairing[0] >= 0, body, empty, *args)


def on_device(queries, key_rows, value_rows, cotangent, norm_gain, pairing):
    width = queries.shape[1]
    heads = width // HD
    group = math.gcd(4, heads)
    steps = heads // group
    features = float(HEADS * HD)
    wide = pl.BlockSpec((BLOCK, group * HD), lambda g: (0, g))
    square = pl.BlockSpec((group, BLOCK, BLOCK), lambda g: (g, 0, 0))
    line = pl.BlockSpec((1, group * HD), lambda g: (0, g))
    whole = pl.BlockSpec((2, BLOCK), lambda g: (0, 0))
    rows_low = jax.ShapeDtypeStruct((BLOCK, width), BF16)
    rows_wide = jax.ShapeDtypeStruct((BLOCK, width), F32)
    weights = jax.ShapeDtypeStruct((heads, BLOCK, BLOCK), BF16)

    def call(body, name, ins, outs, shapes, dots, exps=0, scratch=()):
        return pl.pallas_call(
            body,
            name=name,
            grid=(steps,),
            in_specs=ins,
            out_specs=outs,
            out_shape=shapes,
            scratch_shapes=scratch,
            compiler_params=pltpu.CompilerParams(vmem_limit_bytes=56 * 2**20),
            cost_estimate=pl.CostEstimate(
                flops=dots * heads * 2 * BLOCK * BLOCK * HD,
                bytes_accessed=(len(ins) + 2) * BLOCK * width * 2,
                transcendentals=exps * heads * BLOCK * BLOCK,
            ),
        )

    gain = norm_gain.reshape(1, width)
    index = lax.axis_index("ctx").astype(jnp.int32).reshape(1)
    part = pl.BlockSpec((BLOCK // 2, group * HD), lambda g: (0, g))
    smem = pl.BlockSpec(memory_space=pltpu.SMEM)

    def first_stage(keys, index, pairing):
        return spread(keys), shift(upper(keys), 1), make_plans(index, pairing)

    keys_spread, kp_upper, (plan, plan_back) = stage(
        pairing, first_stage, key_rows, index, pairing
    )
    keys_crossed, (kp_lower, values_spread) = cross(
        keys_spread,
        plan,
        lambda keys, values: (shift(lower(keys), 1), spread(values)),
        (key_rows, value_rows),
    )
    values_crossed, (vp_upper, kt) = cross(
        values_spread,
        plan,
        lambda values, crossed: (shift(upper(values), 1), collect(crossed)),
        (value_rows, keys_crossed),
    )

    def last_stage(crossed, index, q, ko, kt, vo, kp_upper, kp_lower):
        weighed = call(
            functools.partial(scores_kernel, group),
            "scores",
            [smem] + [wide] * 4 + [part] * 2,
            [square] * 3 + [wide],
            [weights] * 3 + [rows_wide],
            4,
            3,
        )(index, q, ko, kt, vo, kp_upper, kp_lower)
        return weighed, collect(crossed), shift(lower(vo), 1)

    (pp, po, pt, acc), vt, vp_lower = stage(
        pairing,
        last_stage,
        values_crossed,
        index,
        queries,
        key_rows,
        kt,
        value_rows,
        kp_upper,
        kp_lower,
    )
    attn, sums = call(
        functools.partial(attn_kernel, group, steps),
        "attn",
        [square, square, wide, wide, wide, line] + [part] * 2,
        [wide, whole],
        [rows_low, jax.ShapeDtypeStruct((2, BLOCK), F32)],
        2,
        scratch=[pltpu.VMEM((BLOCK, HD), F32)] * 2,
    )(pp, pt, vt, acc, cotangent, gain, vp_upper, vp_lower)
    sums = lax.psum(sums, "head")
    dattn, dvt = call(
        functools.partial(dattn_kernel, group, features),
        "dattn",
        [whole, wide, wide, line, square],
        [wide, wide],
        [rows_low] * 2,
        1,
    )(sums, attn, cotangent, gain, pt)

    def first_back(dvt, pp, pt, dattn, attn, vt, kt, q, *near):
        dvp, dkp, dq = call(
            functools.partial(prior_kernel, group),
            "prior",
            [square] + [wide] * 3 + [part] * 4,
            [wide] * 3,
            [rows_low, rows_low, rows_wide],
            4,
        )(pp, dattn, attn, q, *near)
        dkt, dq = call(
            functools.partial(partner_kernel, group),
            "partner",
            [square] + [wide] * 6,
            [wide, wide],
            [rows_low, rows_wide],
            3,
        )(pt, dattn, attn, vt, kt, q, dq)
        return spread(dvt), dvp, dkp, dkt, dq, shift(upper(dvp), -1)

    dvt_spread, dvp, dkp, dkt, dq, dvn_upper = stage(
        pairing,
        first_back,
        dvt,
        pp,
        pt,
        dattn,
        attn,
        vt,
        kt,
        queries,
        vp_upper,
        vp_lower,
        kp_upper,
        kp_lower,
    )
    dvt_crossed, (dvn_lower, dkt_spread) = cross(
        dvt_spread,
        plan_back,
        lambda values, keys: (shift(lower(values), -1), spread(keys)),
        (dvp, dkt),
    )
    dkt_crossed, (dkn_upper, dvt_home) = cross(
        dkt_spread,
        plan_back,
        lambda keys, crossed: (shift(upper(keys), -1), collect(crossed)),
        (dkp, dvt_crossed),
    )

    def finish(*terms):
        return call(finish_kernel, "finish", [wide] * 2 + [part] * 2, wide, rows_low, 0)(*terms)

    def last_back(crossed, sums, po, dattn, attn, vo, ko, q, dq, gain, dkp, *terms):
        dvo, dko, grad_query, mixed = call(
            functools.partial(own_kernel, group, features),
            "own",
            [whole, square] + [wide] * 6 + [line],
            [wide] * 4,
            [rows_low] * 4,
            4,
        )(sums, po, dattn, attn, vo, ko, q, dq, gain)
        grad_value = finish(dvo, *terms)
        return mixed, grad_query, grad_value, dko, collect(crossed), shift(lower(dkp), -1)

    mixed, grad_query, grad_value, dko, dkt_home, dkn_lower = stage(
        pairing,
        last_back,
        dkt_crossed,
        sums,
        po,
        dattn,
        attn,
        value_rows,
        key_rows,
        queries,
        dq,
        gain,
        dkp,
        dvt_home,
        dvn_upper,
        dvn_lower,
    )
    grad_key = finish(dko, dkt_home, dkn_upper, dkn_lower)
    return mixed, grad_query, grad_key, grad_value


def solution(mesh):
    rows = P("ctx", "head")
    return jax.shard_map(
        on_device,
        mesh=mesh,
        in_specs=(rows, rows, rows, rows, P("head"), P()),
        out_specs=(rows, rows, rows, rows),
        check_vma=False,
    )
```
